256 devices in a mesh: expert: 8 (over z_hi, core), dp: 32 (over x, y, z_lo).
Axes of the slice: x: 4, y: 4, z: 8 (z_hi: 4, z_lo: 2; z = z_hi * 2 + z_lo), core: 2. Of those that a mesh axis runs over, the one named last changes fastest.
Arguments:
- tokens: bfloat16 [2048, 3072], P('dp'), may hold values from -6 to 6
- cotangent: bfloat16 [2048, 3072], P('dp'), may hold values from -6 to 6
- expert_ids: int32 [2048, 2], P('dp'), may hold values from 0 to 7, as said below
- gate_values: float32 [2048, 2], P('dp'), may hold values from 0.2 to 1
- w_gate: bfloat16 [8, 8192, 3072], P('expert', 'dp'), may hold values from -0.109375 to 0.109375
- w_up: bfloat16 [8, 8192, 3072], P('expert', 'dp'), may hold values from -0.109375 to 0.109375
- w_down: bfloat16 [8, 8192, 3072], P('expert', 'dp'), may hold values from -0.0625 to 0.0625
Outputs:
- layer_out: bfloat16 [2048, 3072], P('dp')
- input_grad: bfloat16 [2048, 3072], P('dp')
- gate_grad: float32 [2048, 2], P('dp')
- grad_w_gate: bfloat16 [8, 8192, 3072], P('expert', 'dp')
- grad_w_up: bfloat16 [8, 8192, 3072], P('expert', 'dp')
- grad_w_down: bfloat16 [8, 8192, 3072], P('expert', 'dp')
The draws below stay inside these ranges and needn't reach their ends.
Inputs may be any that keep to these rules, and one draw needn't show every extreme that they name: `expert_ids`: each token names two different experts. One expert, the same for all tokens, is named by exactly 32 of the tokens of every index of dp. The remaining entries of each index of dp go to the other experts in a cyclic order from a drawn start, as evenly as possible, so that none of them is named more than 14 times there; which tokens carry which entries is drawn.
All inputs are finite; a program needn't handle non-finite values.
Results may differ from the reference program's by a relative error of at most 0.0059.
Values may be sent and summed in bfloat16 or wider, within the bound.
No kernel may reach another device: no remote copies, remote signals or barrier semaphores. Data moves between devices by JAX's collectives and lax.ppermute only.
A program may use at most 128 MiB of HBM per device.

```python
import jax
import jax.numpy as jnp
from jax import lax

D = 3072
FF = 8192
EXPERTS = 8
TOK_DEV = 64
TOKENS = 2048


def draw_expert_ids(key, part):
    key = jax.random.fold_in(key, 7)
    hot_id = jax.random.randint(jax.random.fold_in(key, 1), (), 0, EXPERTS).astype(jnp.int32)
    block_keys = jax.random.split(jax.random.fold_in(key, 2), TOKENS // TOK_DEV)

    def one_block(block_key):
        key_one, key_two, key_three, key_four = jax.random.split(block_key, 4)
        shuffle = jax.random.permutation(key_one, TOK_DEV).astype(jnp.int32)
        is_hot = shuffle < TOK_DEV // 2
        entries = jnp.where(is_hot, 1, 2).astype(jnp.int32)
        ranking = jax.random.permutation(key_two, TOK_DEV).astype(jnp.int32)
        ordered = entries[ranking]
        starts_ordered = jnp.cumsum(ordered) - ordered
        starts = jnp.zeros((TOK_DEV,), jnp.int32).at[ranking].set(starts_ordered.astype(jnp.int32))
        offset = jax.random.randint(key_three, (), 0, EXPERTS - 1).astype(jnp.int32)
        lead_cold = (offset + starts) % (EXPERTS - 1)
        second = (offset + starts + 1) % (EXPERTS - 1)
        lead_cold = lead_cold + (lead_cold >= hot_id).astype(jnp.int32)
        second = second + (second >= hot_id).astype(jnp.int32)
        swapped = jax.random.randint(key_four, (TOK_DEV,), 0, 2).astype(jnp.int32)
        column_one = jnp.where(is_hot, jnp.where(swapped == 1, hot_id, lead_cold), lead_cold)
        column_two = jnp.where(is_hot, jnp.where(swapped == 1, lead_cold, hot_id), second)
        return jnp.stack([column_one, column_two], axis=1)
    return jax.vmap(one_block)(block_keys).reshape(TOKENS, 2).astype(jnp.int32)


def level_of(rng, dims, shards, least, high):
    def one(axis_at, shards_of):
        draws = jax.random.uniform(jax.random.fold_in(jax.random.fold_in(rng, 6), axis_at), (shards_of,), jnp.float32, least / len(shards), high / len(shards))
        return jnp.repeat(jnp.exp(draws), dims[axis_at] // shards_of).reshape((-1,) + (1,) * (len(dims) - axis_at - 1))

    gain = one(*shards[0])
    for cut in shards[1:]:
        gain = gain * one(*cut)
    return gain


def centred(rng, shape, deviation, most, cuts=(), kind=jnp.bfloat16):
    values = deviation * jax.random.normal(rng, shape, jnp.float32)
    if cuts:
        values = values * level_of(rng, shape, cuts, -0.22, 0.18)
    return jnp.clip(values, -most, most).astype(kind)


def setup_inputs(seed: int = 0) -> dict:
    key_of = jax.random.split(jax.random.key(seed), 8)
    tokens = centred(key_of[0], (TOKENS, D), 1.0, 6.0, ((0, 32),))
    cotangent = centred(key_of[1], (TOKENS, D), 1.0, 6.0, ((0, 32),))
    expert_ids = draw_expert_ids(jax.random.fold_in(key_of[7], 71), 0)
    gate_values = jnp.clip(0.2 + 0.8 * jax.random.uniform(key_of[3], (TOKENS, 2), jnp.float32) ** level_of(key_of[3], (TOKENS, 2), ((0, 32),), -0.2, 0.2), 0.2, 1.0)
    w_gate = centred(key_of[4], (EXPERTS, FF, D), D ** -0.5, 0.109375, ((0, 8), (1, 32)))
    w_up = centred(key_of[5], (EXPERTS, FF, D), D ** -0.5, 0.109375, ((0, 8), (1, 32)))
    w_down = centred(key_of[6], (EXPERTS, FF, D), FF ** -0.5, 0.0625, ((0, 8), (1, 32)))
    return {"tokens": tokens, "cotangent": cotangent, "expert_ids": expert_ids, "gate_values": gate_values, "w_gate": w_gate, "w_up": w_up, "w_down": w_down}


def reference(tokens, cotangent, expert_ids, gate_values, w_gate, w_up, w_down):
    capacity = TOKENS // 2

    def one_expert(expert):
        matches = expert_ids == expert
        routed = jnp.any(matches, axis=1)
        weight = jnp.sum(jnp.where(matches, gate_values, 0.0), axis=1)
        ranking = jnp.argsort(jnp.where(routed, 0, 1).astype(jnp.int32), stable=True)[:capacity]
        live = routed[ranking].astype(jnp.float32)
        selected = tokens[ranking]
        gate_matrix = w_gate[expert]
        up_matrix = w_up[expert]
        down_matrix = w_down[expert]
        gate_pre = jnp.dot(selected, gate_matrix.T, preferred_element_type=jnp.float32)
        up_pre = jnp.dot(selected, up_matrix.T, preferred_element_type=jnp.float32)
        sigma = jax.nn.sigmoid(gate_pre)
        activation = gate_pre * sigma
        hidden = (activation * up_pre).astype(jnp.bfloat16)
        out_rows = jnp.dot(hidden, down_matrix, preferred_element_type=jnp.float32) * live[:, None]
        row_gate = weight[ranking] * live
        out_grad = (row_gate[:, None] * cotangent[ranking].astype(jnp.float32)).astype(jnp.bfloat16)
        hidden_grad = jnp.dot(out_grad, down_matrix.T, preferred_element_type=jnp.float32)
        gate_grad_pre = (hidden_grad * up_pre * sigma * (1.0 + gate_pre * (1.0 - sigma))).astype(jnp.bfloat16)
        up_grad_pre = (hidden_grad * activation).astype(jnp.bfloat16)
        grad_rows = jnp.dot(gate_grad_pre, gate_matrix, preferred_element_type=jnp.float32)
        grad_rows = grad_rows + jnp.dot(up_grad_pre, up_matrix, preferred_element_type=jnp.float32)
        grad_gate = jnp.dot(gate_grad_pre.T, selected, preferred_element_type=jnp.float32).astype(jnp.bfloat16)
        grad_up = jnp.dot(up_grad_pre.T, selected, preferred_element_type=jnp.float32).astype(jnp.bfloat16)
        grad_down = jnp.dot(hidden.T, out_grad, preferred_element_type=jnp.float32).astype(jnp.bfloat16)
        empty = jnp.zeros((TOKENS, D), jnp.float32)
        out_part = empty.at[ranking].add(row_gate[:, None] * out_rows)
        out_tokens = empty.at[ranking].add(out_rows)
        grad_part = empty.at[ranking].add(grad_rows * live[:, None])
        inner = jnp.sum(cotangent.astype(jnp.float32) * out_tokens, axis=1)
        gate_part = jnp.where(matches, inner[:, None], 0.0)
        return out_part, grad_part, gate_part, grad_gate, grad_up, grad_down

    pieces = lax.map(one_expert, jnp.arange(EXPERTS, dtype=jnp.int32))
    layer_out = jnp.sum(pieces[0], axis=0).astype(jnp.bfloat16)
    input_grad = jnp.sum(pieces[1], axis=0).astype(jnp.bfloat16)
    gate_grad = jnp.sum(pieces[2], axis=0)
    return layer_out, input_grad, gate_grad, pieces[3], pieces[4], pieces[5]
```

```python
import jax
import jax.numpy as jnp
from jax import lax
from jax.sharding import PartitionSpec as P

BF = jnp.bfloat16
F32 = jnp.float32
ZH, CORES, NX, NY, ZL = 4, 2, 4, 4, 2
BOTH = ("expert", "dp")


def linear(zh, core, x, y, zl):
    return (((zh * CORES + core) * NX + x) * NY + y) * ZL + zl


def moves(step):
    pairs = []
    for zh in range(ZH):
        for core in range(CORES):
            for x in range(NX):
                for y in range(NY):
                    for zl in range(ZL):
                        tx, ty, tz = step(core, x, y, zl)
                        pairs.append((linear(zh, core, x, y, zl), linear(zh, core, tx, ty, tz)))
    return pairs


def along(first, shift):
    def step(core, x, y, zl):
        if (core == 0) == first:
            return ((x + shift) % NX, y, zl)
        return (x, (y + shift) % NY, zl)

    return moves(step)


TWIN = moves(lambda core, x, y, zl: (x, y, 1 - zl))
FIRST_UP, FIRST_DOWN = along(True, 1), along(True, -1)
SECOND_UP, SECOND_DOWN = along(False, 1), along(False, -1)


def send(value, pairs):
    return lax.ppermute(value, BOTH, pairs)


def dot_nt(a, b):
    return lax.dot_general(a, b, (((1,), (1,)), ((), ())), preferred_element_type=F32)


def dot_nn(a, b):
    return lax.dot_general(a, b, (((1,), (0,)), ((), ())), preferred_element_type=F32)


def dot_tn(a, b):
    return lax.dot_general(a, b, (((0,), (0,)), ((), ())), preferred_element_type=F32)


def gather_second(rows):
    n = rows.shape[0] // 2
    a, b = rows[:n], rows[n:]
    left_b, right_a = send(b, SECOND_UP), send(a, SECOND_DOWN)
    left_a, right_b = send(a, SECOND_UP), send(b, SECOND_DOWN)
    far_b, far_a = send(left_b, SECOND_UP), send(right_a, SECOND_DOWN)
    return [a, b, left_a, left_b, right_a, right_b, far_a, far_b]


def scatter_rows(partial, slots):
    far_a, far_b = partial(6).astype(BF), partial(7).astype(BF)
    to_right_a, to_left_b = send(far_a, SECOND_UP), send(far_b, SECOND_DOWN)
    from_left_b = send(partial(5).astype(BF), SECOND_UP)
    from_right_a = send(partial(2).astype(BF), SECOND_DOWN)
    from_left_a = send((partial(4) + to_right_a.astype(F32)).astype(BF), SECOND_UP)
    from_right_b = send((partial(3) + to_left_b.astype(F32)).astype(BF), SECOND_DOWN)
    part_a = partial(0) + from_left_a.astype(F32) + from_right_a.astype(F32)
    part_b = partial(1) + from_left_b.astype(F32) + from_right_b.astype(F32)
    far, left = part_a[: 2 * slots], part_a[2 * slots :]
    right, own = part_b[: 2 * slots], part_b[2 * slots :]
    far = far.astype(BF)
    to_right = send(far[:slots], FIRST_UP)
    to_left = send(far[slots:], FIRST_DOWN)
    right = jnp.concatenate([right[:slots] + to_right.astype(F32), right[slots:]])
    left = jnp.concatenate([left[:slots], left[slots:] + to_left.astype(F32)])
    from_left = send(right.astype(BF), FIRST_UP)
    from_right = send(left.astype(BF), FIRST_DOWN)
    own = own + from_left.astype(F32) + from_right.astype(F32)
    return own[:slots] + send(own[slots:].astype(BF), TWIN).astype(F32)


def combine(term):
    shares = lax.all_to_all(term.astype(BF), "expert", 0, 0, tiled=True)
    shares = shares.reshape(ZH * CORES, -1, term.shape[1]).astype(F32)
    return lax.all_gather(jnp.sum(shares, axis=0).astype(BF), "expert", axis=0, tiled=True)


def on_device(tokens, cotangent, expert_ids, gate_values, w_gate, w_up, w_down):
    w_gate, w_up, w_down = w_gate[0], w_up[0], w_down[0]
    slots = tokens.shape[0] // 2
    mine = lax.axis_index("expert")
    matches = expert_ids == mine
    routed = jnp.any(matches, axis=1)
    weight = jnp.sum(jnp.where(matches, gate_values, 0.0), axis=1)
    position = jnp.cumsum(routed.astype(jnp.int32)) - 1
    placing = routed[:, None] & (position[:, None] == jnp.arange(slots, dtype=jnp.int32)[None, :])
    placing = placing.astype(BF)
    scaled = (weight[:, None] * cotangent.astype(F32)).astype(BF)
    row_inputs = dot_tn(placing, tokens).astype(BF)
    row_grads = dot_tn(placing, scaled).astype(BF)

    own = jnp.stack([row_inputs, row_grads])
    twin = send(own, TWIN)
    own = jnp.concatenate([own, twin], axis=1)
    left, right = send(own, FIRST_UP), send(own, FIRST_DOWN)
    far_inputs, far_grads = send(right[0], FIRST_DOWN), send(left[1], FIRST_UP)
    inputs = gather_second(jnp.concatenate([far_inputs, left[0], right[0], own[0]]))
    grads = gather_second(jnp.concatenate([far_grads, left[1], right[1], own[1]]))

    gate_pre = [dot_nt(x, w_gate) for x in inputs]
    up_pre = [dot_nt(x, w_up) for x in inputs]
    sigma = [jax.nn.sigmoid(g) for g in gate_pre]
    hidden = [(g * s * u).astype(BF) for g, s, u in zip(gate_pre, sigma, up_pre)]
    out_rows = scatter_rows(lambda i: dot_nn(hidden[i], w_down), slots)

    gate_grad_pre, up_grad_pre = [], []
    for x, g, s, u in zip(grads, gate_pre, sigma, up_pre):
        h = dot_nt(x, w_down)
        gate_grad_pre.append((h * u * s * (1.0 + g * (1.0 - s))).astype(BF))
        up_grad_pre.append((h * (g * s)).astype(BF))
    grad_rows = scatter_rows(
        lambda i: dot_nn(gate_grad_pre[i], w_gate) + dot_nn(up_grad_pre[i], w_up), slots
    )

    all_inputs, all_grads = jnp.concatenate(inputs), jnp.concatenate(grads)
    grad_gate = dot_tn(jnp.concatenate(gate_grad_pre), all_inputs).astype(BF)
    grad_up = dot_tn(jnp.concatenate(up_grad_pre), all_inputs).astype(BF)
    grad_down = dot_tn(jnp.concatenate(hidden), all_grads).astype(BF)

    index = jnp.clip(position, 0, slots - 1)[:, None]
    live = routed[:, None].astype(F32)
    out_tokens = jnp.take_along_axis(out_rows, index, axis=0) * live
    grad_tokens = jnp.take_along_axis(grad_rows, index, axis=0) * live
    layer_out = combine(weight[:, None] * out_tokens)
    inner = jnp.sum(cotangent.astype(F32) * out_tokens, axis=1)
    gate_term = jnp.where(matches, inner[:, None], 0.0)
    gate_grad = jnp.sum(lax.all_gather(gate_term, "expert"), axis=0)
    input_grad = combine(grad_tokens)
    return layer_out, input_grad, gate_grad, grad_gate[None], grad_up[None], grad_down[None]


def solution(mesh):
    rows = P("dp", None)
    weights = P("expert", "dp", None)
    return jax.shard_map(
        on_device,
        mesh=mesh,
        in_specs=(rows, rows, rows, rows, weights, weights, weights),
        out_specs=(rows, rows, rows, weights, weights, weights),
        check_vma=False,
    )
```

```python
import jax
import jax.numpy as jnp
from jax import lax
from jax.sharding import PartitionSpec as P

BF = jnp.bfloat16
F32 = jnp.float32
ZH, CORES, NX, NY, ZL = 4, 2, 4, 4, 2
BOTH = ("expert", "dp")
BASE, OVER = 16, 8
SLOTS = BASE + OVER
CELL, CUT = 2 * SLOTS, 2 * BASE


def linear(zh, core, x, y, zl):
    return (((zh * CORES + core) * NX + x) * NY + y) * ZL + zl


def moves(step):
    pairs = []
    for zh in range(ZH):
        for core in range(CORES):
            for x in range(NX):
                for y in range(NY):
                    for zl in range(ZL):
                        at = (zh, core, x, y, zl)
                        pairs.append((linear(*at), linear(*step(*at))))
    return pairs


def along(first, shift):
    def step(zh, core, x, y, zl):
        if (core == 0) == first:
            return (zh, core, (x + shift) % NX, y, zl)
        return (zh, core, x, (y + shift) % NY, zl)

    return moves(step)


def planes(shift):
    return moves(lambda zh, core, x, y, zl: ((zh + shift) % ZH, core, x, y, zl))


TWIN = moves(lambda zh, core, x, y, zl: (zh, core, x, y, 1 - zl))
CORE = moves(lambda zh, core, x, y, zl: (zh, 1 - core, x, y, zl))
FIRST_UP, FIRST_DOWN = along(True, 1), along(True, -1)
SECOND_UP, SECOND_DOWN = along(False, 1), along(False, -1)


def send(value, pairs, name):
    with jax.named_scope(name):
        return lax.ppermute(value, BOTH, pairs)


def dot_nt(a, b):
    return lax.dot_general(a, b, (((1,), (1,)), ((), ())), preferred_element_type=F32)


def dot_nn(a, b):
    return lax.dot_general(a, b, (((1,), (0,)), ((), ())), preferred_element_type=F32)


def dot_tn(a, b):
    return lax.dot_general(a, b, (((0,), (0,)), ((), ())), preferred_element_type=F32)


def exact(a, b):
    return jnp.dot(a, b, preferred_element_type=F32, precision=lax.Precision.HIGHEST)


def join(own, twin):
    return jnp.concatenate([own[:, :BASE], twin[:, :BASE], own[:, BASE:], twin[:, BASE:]], axis=1)


def split(cell):
    own = jnp.concatenate([cell[:, :BASE], cell[:, CUT : CUT + OVER]], axis=1)
    twin = jnp.concatenate([cell[:, BASE:CUT], cell[:, CUT + OVER :]], axis=1)
    return own, twin


def tie(value, *others):
    return lax.optimization_barrier((value, *others))[0]


def on_device(tokens, cotangent, expert_ids, gate_values, w_gate, w_up, w_down):
    w_gate, w_up, w_down = w_gate[0], w_up[0], w_down[0]
    count = tokens.shape[0]
    mine = lax.axis_index("expert")
    core, plane = mine % CORES, mine // CORES
    pair = jnp.stack([mine, mine + 1 - 2 * core])
    matches = expert_ids[:, None, :] == pair[None, :, None]
    routed = jnp.any(matches, axis=2)
    weight = jnp.sum(jnp.where(matches, gate_values[:, None, :], 0.0), axis=2)
    position = jnp.cumsum(routed.astype(jnp.int32), axis=0) - 1
    hot = (position[-1, 0] >= BASE).astype(F32)
    base_slots = jnp.arange(BASE, dtype=jnp.int32)
    over_slots = BASE + OVER * core + jnp.arange(OVER, dtype=jnp.int32)
    none = jnp.zeros((count, BASE), bool)
    placing = [
        jnp.concatenate(
            [
                (routed[:, j, None] & (position[:, j, None] == base_slots)) if j == 0 else none,
                routed[:, j, None] & (position[:, j, None] == over_slots),
            ],
            axis=1,
        )
        for j in range(2)
    ]
    placed = (placing[0] | placing[1]).astype(BF)
    slot_weight = sum(jnp.sum(jnp.where(placing[j], weight[:, j, None], 0.0), axis=0) for j in range(2))
    row_inputs = dot_tn(placed, tokens).astype(BF)
    row_grads = (slot_weight[:, None] * dot_tn(placed, cotangent)).astype(BF)

    w_both = jnp.concatenate([w_gate, w_up])
    own = jnp.stack([row_inputs, row_grads])
    own = join(own, send(own, TWIN, "twin"))
    left, right = send(own, FIRST_UP, "first_left"), send(own, FIRST_DOWN, "first_right")
    far_x, far_g = send(right[0], FIRST_DOWN, "first_far_inputs"), send(left[1], FIRST_UP, "first_far_grads")
    own_x = jnp.stack([far_x, left[0], right[0], own[0]])
    own_g = jnp.stack([far_g, left[1], right[1], own[1]])
    left_x, right_x = send(own_x, SECOND_UP, "inputs_left"), send(own_x, SECOND_DOWN, "inputs_right")
    def rows_of(cells):
        return cells.reshape(-1, cells.shape[-1])

    def forward(rows, cells):
        live = hot
        if cells:
            live = jnp.where(jnp.arange(rows.shape[0])[:, None] % CELL < CUT, 1.0, hot)
        g, u = jnp.split(dot_nt(rows, w_both), 2, axis=1)
        s = jax.nn.sigmoid(g)
        return live, g, u, s, (live * (g * s * u)).astype(BF)

    def backward(rows, live, g, u, s, hidden):
        h = live * dot_nt(rows, w_down)
        return hidden, jnp.concatenate([h * u * s * (1.0 + g * (1.0 - s)), h * (g * s)], axis=1).astype(BF)

    def partial(result, lo, hi):
        hidden, pre = result
        return dot_nn(hidden[lo:hi], w_down), dot_nn(pre[lo:hi], w_both)

    def others_of(inputs, grads, name):
        mine = jnp.stack([rows_of(jnp.concatenate([c[:, CUT:] for c in v])) for v in (inputs, grads)])
        return send(mine, CORE, name + "_core")

    def swap(mine, name):
        return send(mine, CORE, name + "_core_back").reshape(2, -1, CELL - CUT, mine.shape[-1])

    def below(rows):
        return jnp.pad(rows.astype(F32), ((0, 0), (CUT, 0), (0, 0)))

    own_f = forward(rows_of(own_x), True)
    own_g = tie(own_g, own_f[4])
    left_g, right_g = send(own_g, SECOND_UP, "grads_left"), send(own_g, SECOND_DOWN, "grads_right")
    far_x = send(tie(right_x[:2], own_g), SECOND_DOWN, "inputs_far"), send(tie(left_x[2:], own_g), SECOND_UP, "inputs_far")

    left_g, right_g = tie(left_g, *far_x), tie(right_g, *far_x)
    near_x, near_g = (own_x, left_x, right_x), (own_g, left_g, right_g)
    near_f = [own_f] + [forward(rows_of(x), True) for x in near_x[1:]]
    hiddens = [f[4] for f in near_f]
    far_g = (
        send(tie(right_g[:2], *hiddens), SECOND_DOWN, "grads_far"),
        send(tie(left_g[2:], *hiddens), SECOND_UP, "grads_far"),
    )
    over = others_of(near_x, near_g, "near")
    near_b = [backward(rows_of(g), *f) for g, f in zip(near_g, near_f)]
    over_b = backward(over[1], *forward(over[0], False))
    near_mine = jnp.stack([v.astype(BF) for v in partial(over_b, None, None)])
    near_s = swap(near_mine, "near")

    def piece(block, lo):
        return [
            v.reshape(2, CELL, -1) + below(near_s[a, 4 * block + lo : 4 * block + lo + 2])
            for a, v in enumerate(partial(near_b[block], lo * CELL, (lo + 2) * CELL))
        ]

    right_b = jnp.stack(piece(2, 2)).astype(BF)
    left_a = jnp.stack(piece(1, 0)).astype(BF)
    from_left_b, from_right_a = send(right_b, SECOND_UP, "right_sums"), send(left_a, SECOND_DOWN, "left_sums")

    far_x, far_g = (tie(jnp.concatenate(v), near_s) for v in (far_x, far_g))
    far_over = others_of((far_x,), (far_g,), "far")
    far_x, far_g = rows_of(far_x), rows_of(far_g)
    far_over_b = backward(far_over[1], *forward(far_over[0], False))
    far_s = swap(jnp.stack([v.astype(BF) for v in partial(far_over_b, None, None)]), "far")
    far_b = backward(far_g, *forward(far_x, True))
    far_sums = [v.reshape(4, CELL, -1) + below(far_s[a]) for a, v in enumerate(partial(far_b, None, None))]
    everything = [*near_b, over_b, far_b, far_over_b]
    far_a, far_b = (jnp.stack([v[lo : lo + 2] for v in far_sums]).astype(BF) for lo in (0, 2))
    far_a, far_b = tie(far_a, from_left_b, from_right_a), tie(far_b, from_left_b, from_right_a)
    to_right = send(far_a, SECOND_UP, "far_sums").astype(F32)
    to_left = send(far_b, SECOND_DOWN, "far_sums").astype(F32)
    right_a = jnp.stack([v + to_right[a] for a, v in enumerate(piece(2, 0))]).astype(BF)
    left_b = jnp.stack([v + to_left[a] for a, v in enumerate(piece(1, 2))]).astype(BF)
    from_left_a, from_right_b = send(right_a, SECOND_UP, "right_sums"), send(left_b, SECOND_DOWN, "left_sums")

    hidden, pre = (tie(jnp.concatenate([r[a] for r in everything]), to_right, to_left) for a in range(2))
    all_inputs = jnp.concatenate([*map(rows_of, near_x), over[0], far_x, far_over[0]])
    all_grads = jnp.concatenate([*map(rows_of, near_g), over[1], far_g, far_over[1]])
    grad_down = dot_tn(hidden, all_grads).astype(BF)
    grad_gate = dot_tn(pre[:, : w_gate.shape[0]], all_inputs).astype(BF)
    grad_up = dot_tn(pre[:, w_gate.shape[0] :], all_inputs).astype(BF)

    sum_a = [v + from_left_a[a].astype(F32) + from_right_a[a].astype(F32) for a, v in enumerate(piece(0, 0))]
    sum_b = [v + from_left_b[a].astype(F32) + from_right_b[a].astype(F32) for a, v in enumerate(piece(0, 2))]
    to_right = send(sum_a[0][0].astype(BF), FIRST_UP, "first_far_sums").astype(F32)
    to_left = send(sum_a[1][0].astype(BF), FIRST_DOWN, "first_far_sums").astype(F32)
    right = jnp.stack([sum_b[0][0] + to_right, sum_b[1][0]]).astype(BF)
    left = jnp.stack([sum_a[0][1], sum_a[1][1] + to_left]).astype(BF)
    from_left, from_right = send(right, FIRST_UP, "first_right_sums"), send(left, FIRST_DOWN, "first_left_sums")
    own_sum = jnp.stack([sum_b[0][1], sum_b[1][1]]) + from_left.astype(F32) + from_right.astype(F32)
    own_sum, twin_sum = split(own_sum)
    twin_sum = tie(twin_sum.astype(BF), grad_down, grad_gate, grad_up)
    out_rows, grad_rows = own_sum + send(twin_sum, TWIN, "twin_sums").astype(F32)

    part = count // (CORES * ZH)
    column = jnp.arange(count, dtype=jnp.int32)
    their_core = (core + column // (part * ZH)) % CORES
    their_plane = (plane + column // part) % ZH
    token = (their_core * ZH + their_plane) * part + column % part
    to_place = (jnp.arange(count, dtype=jnp.int32)[:, None] == token[None, :]).astype(BF)
    choose = dot_tn(to_place, placed)
    inner = exact(cotangent.astype(F32), out_rows.T)
    gate_grad = sum(
        jnp.where(matches[:, j, :], jnp.sum(jnp.where(placing[j], inner, 0.0), axis=1)[:, None], 0.0)
        for j in range(2)
    )
    high = lax.reduce_precision(gate_grad, 8, 7)
    parts = jnp.concatenate([high, gate_grad - high], axis=1).astype(BF)
    parts = jnp.pad(dot_tn(to_place, parts), ((0, 0), (0, 128 - 4)))
    term = jnp.stack(
        [
            jnp.concatenate([exact(choose * slot_weight, out_rows), parts], axis=1),
            jnp.concatenate([exact(choose, grad_rows), jnp.zeros_like(parts)], axis=1),
        ]
    )
    half = count // CORES
    term = term[:, :half] + send(term[:, half:].astype(BF), CORE, "core_sum").astype(F32)
    low, total = term.astype(BF), term[:, :part]
    for s in range(1, ZH):
        total = total + send(low[:, s * part : (s + 1) * part], planes(s), "planes_sum").astype(F32)
    total = total.astype(BF)
    term = jnp.concatenate([total] + [send(total, planes(-s), "planes") for s in range(1, ZH)], axis=1)
    term = jnp.concatenate([term, send(term, CORE, "core")], axis=1)
    width = tokens.shape[1]
    layer_out, input_grad = (dot_nn(to_place, term[a, :, :width]).astype(BF) for a in range(2))
    parts = dot_nn(to_place, term[0, :, width:])
    gate_grad = parts[:, :2] + parts[:, 2:4]
    return layer_out, input_grad, gate_grad, grad_gate[None], grad_up[None], grad_down[None]


def solution(mesh):
    rows = P("dp", None)
    weights = P("expert", "dp", None)
    return jax.shard_map(
        on_device,
        mesh=mesh,
        in_specs=(rows, rows, rows, rows, weights, weights, weights),
        out_specs=(rows, rows, rows, weights, weights, weights),
        check_vma=False,
    )
```

```python
import jax
import jax.numpy as jnp
from jax import lax
from jax.sharding import PartitionSpec as P

BF = jnp.bfloat16
F32 = jnp.float32
ZH, CORES, NX, NY, ZL = 4, 2, 4, 4, 2
BOTH = ("expert", "dp")
BASE, OVER = 16, 8
SLOTS = BASE + OVER
CELL, CUT = 2 * SLOTS, 2 * BASE


def linear(zh, core, x, y, zl):
    return (((zh * CORES + core) * NX + x) * NY + y) * ZL + zl


def moves(step):
    pairs = []
    for zh in range(ZH):
        for core in range(CORES):
            for x in range(NX):
                for y in range(NY):
                    for zl in range(ZL):
                        at = (zh, core, x, y, zl)
                        pairs.append((linear(*at), linear(*step(*at))))
    return pairs


def along(first, shift):
    def step(zh, core, x, y, zl):
        if (core == 0) == first:
            return (zh, core, (x + shift) % NX, y, zl)
        return (zh, core, x, (y + shift) % NY, zl)

    return moves(step)


def planes(shift):
    return moves(lambda zh, core, x, y, zl: ((zh + shift) % ZH, core, x, y, zl))


TWIN = moves(lambda zh, core, x, y, zl: (zh, core, x, y, 1 - zl))
CORE = moves(lambda zh, core, x, y, zl: (zh, 1 - core, x, y, zl))
FIRST_UP, FIRST_DOWN = along(True, 1), along(True, -1)
SECOND_UP, SECOND_DOWN = along(False, 1), along(False, -1)


def send(value, pairs, name):
    with jax.named_scope(name):
        return lax.ppermute(value, BOTH, pairs)


def dot_nt(a, b):
    return lax.dot_general(a, b, (((1,), (1,)), ((), ())), preferred_element_type=F32)


def dot_nn(a, b):
    return lax.dot_general(a, b, (((1,), (0,)), ((), ())), preferred_element_type=F32)


def dot_tn(a, b):
    return lax.dot_general(a, b, (((0,), (0,)), ((), ())), preferred_element_type=F32)


def exact(a, b):
    return jnp.dot(a, b, preferred_element_type=F32, precision=lax.Precision.HIGHEST)


def join(own, twin):
    return jnp.concatenate([own[:, :BASE], twin[:, :BASE], own[:, BASE:], twin[:, BASE:]], axis=1)


def split(cell):
    own = jnp.concatenate([cell[:, :BASE], cell[:, CUT : CUT + OVER]], axis=1)
    twin = jnp.concatenate([cell[:, BASE:CUT], cell[:, CUT + OVER :]], axis=1)
    return own, twin


def tie(value, *others):
    return lax.optimization_barrier((value, *others))[0]


def on_device(tokens, cotangent, expert_ids, gate_values, w_gate, w_up, w_down):
    w_gate, w_up, w_down = w_gate[0], w_up[0], w_down[0]
    count = tokens.shape[0]
    mine = lax.axis_index("expert")
    core, plane = mine % CORES, mine // CORES
    pair = jnp.stack([mine, mine + 1 - 2 * core])
    matches = expert_ids[:, None, :] == pair[None, :, None]
    routed = jnp.any(matches, axis=2)
    weight = jnp.sum(jnp.where(matches, gate_values[:, None, :], 0.0), axis=2)
    position = jnp.cumsum(routed.astype(jnp.int32), axis=0) - 1
    hot = (position[-1, 0] >= BASE).astype(F32)
    base_slots = jnp.arange(BASE, dtype=jnp.int32)
    over_slots = BASE + OVER * core + jnp.arange(OVER, dtype=jnp.int32)
    none = jnp.zeros((count, BASE), bool)
    placing = [
        jnp.concatenate(
            [
                (routed[:, j, None] & (position[:, j, None] == base_slots)) if j == 0 else none,
                routed[:, j, None] & (position[:, j, None] == over_slots),
            ],
            axis=1,
        )
        for j in range(2)
    ]
    placed = (placing[0] | placing[1]).astype(BF)
    slot_weight = sum(jnp.sum(jnp.where(placing[j], weight[:, j, None], 0.0), axis=0) for j in range(2))
    row_inputs = dot_tn(placed, tokens).astype(BF)
    row_grads = (slot_weight[:, None] * dot_tn(placed, cotangent)).astype(BF)

    w_both = jnp.concatenate([w_gate, w_up])
    own = jnp.stack([row_inputs, row_grads])
    own = join(own, send(own, TWIN, "twin"))
    left, right = send(own, FIRST_UP, "first_left"), send(own, FIRST_DOWN, "first_right")
    far_x, far_g = send(right[0], FIRST_DOWN, "first_far_inputs"), send(left[1], FIRST_UP, "first_far_grads")
    own_a = jnp.stack([jnp.stack([f, left[a]]) for a, f in enumerate((far_x, far_g))])
    own_b = jnp.stack([right, own], axis=1)
    left_b, right_a = send(own_b, SECOND_UP, "left_b"), send(own_a, SECOND_DOWN, "right_a")
    left_a, right_b = send(own_a, SECOND_UP, "left_a"), send(own_b, SECOND_DOWN, "right_b")
    far_a, far_b = send(right_a, SECOND_DOWN, "far_a"), send(left_b, SECOND_UP, "far_b")

    def rows_of(cells):
        return cells.reshape(-1, cells.shape[-1])

    def forward(rows, cells):
        live = hot
        if cells:
            live = jnp.where(jnp.arange(rows.shape[0])[:, None] % CELL < CUT, 1.0, hot)
        g, u = jnp.split(dot_nt(rows, w_both), 2, axis=1)
        s = jax.nn.sigmoid(g)
        return live, g, u, s, (live * (g * s * u)).astype(BF)

    def backward(rows, live, g, u, s, hidden):
        h = live * dot_nt(rows, w_down)
        return hidden, jnp.concatenate([h * u * s * (1.0 + g * (1.0 - s)), h * (g * s)], axis=1).astype(BF)

    def partial(result):
        hidden, pre = result
        return dot_nn(hidden, w_down), dot_nn(pre, w_both)

    def others_of(inputs, grads, name):
        mine = jnp.stack([rows_of(jnp.concatenate([c[:, CUT:] for c in v])) for v in (inputs, grads)])
        return send(mine, CORE, name + "_core")

    def swap(mine, name):
        return send(mine, CORE, name + "_core_back").reshape(2, -1, CELL - CUT, mine.shape[-1])

    def below(rows):
        return jnp.pad(rows.astype(F32), ((0, 0), (CUT, 0), (0, 0)))

    near_x, near_g = zip(own_a, own_b, left_a, left_b, right_b, right_a)
    near_f = [forward(rows_of(x), True) for x in near_x]
    over = others_of(near_x[:5], near_g[:5], "near")
    near_b = [backward(rows_of(g), *f) for g, f in zip(near_g, near_f)]
    over_b = backward(over[1], *forward(over[0], False))
    near_mine = jnp.stack([v.astype(BF) for v in partial(over_b)])
    near_s = swap(near_mine, "near")

    def piece(half):
        return [
            v.reshape(2, CELL, -1) + below(near_s[a, 2 * half : 2 * half + 2] if half < 5 else far_s[a, :2])
            for a, v in enumerate(partial(near_b[half]))
        ]

    right_b = jnp.stack(piece(4)).astype(BF)
    left_a = jnp.stack(piece(2)).astype(BF)
    from_left_b, from_right_a = send(right_b, SECOND_UP, "right_sums"), send(left_a, SECOND_DOWN, "left_sums")

    far_a, far_b = tie(far_a, near_s, right_b, left_a), tie(far_b, near_s, right_b, left_a)
    far_x, far_g = zip(far_a, far_b)
    far_over = others_of((near_x[5], *far_x), (near_g[5], *far_g), "far")
    far_over_b = backward(far_over[1], *forward(far_over[0], False))
    far_s = swap(jnp.stack([v.astype(BF) for v in partial(far_over_b)]), "far")
    far_blocks = [backward(rows_of(g), *forward(rows_of(x), True)) for x, g in zip(far_x, far_g)]
    everything = [*near_b, over_b, *far_blocks, far_over_b]
    to_right, to_left, from_left_a, from_right_b = [], [], [], []
    for a in range(2):
        sums = [
            (partial(far_blocks[h])[a].reshape(2, CELL, -1) + below(far_s[a, 2 * h + 2 : 2 * h + 4])).astype(BF)
            for h in range(2)
        ]
        sums = [tie(v, from_left_b, from_right_a) for v in sums]
        to_right.append(send(sums[0], SECOND_UP, "far_sums"))
        to_left.append(send(sums[1], SECOND_DOWN, "far_sums"))
    for a in range(2):
        right_a = (piece(5)[a] + to_right[a].astype(F32)).astype(BF)
        left_b = (piece(3)[a] + to_left[a].astype(F32)).astype(BF)
        from_left_a.append(send(right_a, SECOND_UP, "right_sums"))
        from_right_b.append(send(left_b, SECOND_DOWN, "left_sums"))

    hidden, pre = (tie(jnp.concatenate([r[a] for r in everything]), *to_right, *to_left) for a in range(2))
    all_inputs = jnp.concatenate([*map(rows_of, near_x), over[0], *map(rows_of, far_x), far_over[0]])
    all_grads = jnp.concatenate([*map(rows_of, near_g), over[1], *map(rows_of, far_g), far_over[1]])
    grad_down = dot_tn(hidden, all_grads).astype(BF)
    grad_gate = dot_tn(pre[:, : w_gate.shape[0]], all_inputs).astype(BF)
    grad_up = dot_tn(pre[:, w_gate.shape[0] :], all_inputs).astype(BF)

    sum_a = [v + from_left_a[a].astype(F32) + from_right_a[a].astype(F32) for a, v in enumerate(piece(0))]
    sum_b = [v + from_left_b[a].astype(F32) + from_right_b[a].astype(F32) for a, v in enumerate(piece(1))]
    to_right = send(sum_a[0][0].astype(BF), FIRST_UP, "first_far_sums").astype(F32)
    to_left = send(sum_a[1][0].astype(BF), FIRST_DOWN, "first_far_sums").astype(F32)
    right = jnp.stack([sum_b[0][0] + to_right, sum_b[1][0]]).astype(BF)
    left = jnp.stack([sum_a[0][1], sum_a[1][1] + to_left]).astype(BF)
    from_left, from_right = send(right, FIRST_UP, "first_right_sums"), send(left, FIRST_DOWN, "first_left_sums")
    own_sum = jnp.stack([sum_b[0][1], sum_b[1][1]]) + from_left.astype(F32) + from_right.astype(F32)
    own_sum, twin_sum = split(own_sum)
    twin_sum = tie(twin_sum.astype(BF), grad_down, grad_gate, grad_up)
    out_rows, grad_rows = own_sum + send(twin_sum, TWIN, "twin_sums").astype(F32)

    part = count // (CORES * ZH)
    column = jnp.arange(count, dtype=jnp.int32)
    their_core = (core + column // (part * ZH)) % CORES
    their_plane = (plane + column // part) % ZH
    token = (their_core * ZH + their_plane) * part + column % part
    to_place = (jnp.arange(count, dtype=jnp.int32)[:, None] == token[None, :]).astype(BF)
    choose = dot_tn(to_place, placed)
    inner = exact(cotangent.astype(F32), out_rows.T)
    gate_grad = sum(
        jnp.where(matches[:, j, :], jnp.sum(jnp.where(placing[j], inner, 0.0), axis=1)[:, None], 0.0)
        for j in range(2)
    )
    high = lax.reduce_precision(gate_grad, 8, 7)
    parts = jnp.concatenate([high, gate_grad - high], axis=1).astype(BF)
    parts = jnp.pad(dot_tn(to_place, parts), ((0, 0), (0, 128 - 4)))
    term = jnp.stack(
        [
            jnp.concatenate([exact(choose * slot_weight, out_rows), parts], axis=1),
            jnp.concatenate([exact(choose, grad_rows), jnp.zeros_like(parts)], axis=1),
        ]
    )
    half = count // CORES
    term = term[:, :half] + send(term[:, half:].astype(BF), CORE, "core_sum").astype(F32)
    low, total = term.astype(BF), term[:, :part]
    for s in range(1, ZH):
        total = total + send(low[:, s * part : (s + 1) * part], planes(s), "planes_sum").astype(F32)
    total = total.astype(BF)
    term = jnp.concatenate([total] + [send(total, planes(-s), "planes") for s in range(1, ZH)], axis=1)
    term = jnp.concatenate([term, send(term, CORE, "core")], axis=1)
    width = tokens.shape[1]
    layer_out, input_grad = (dot_nn(to_place, term[a, :, :width]).astype(BF) for a in range(2))
    parts = dot_nn(to_place, term[0, :, width:])
    gate_grad = parts[:, :2] + parts[:, 2:4]
    return layer_out, input_grad, gate_grad, grad_gate[None], grad_up[None], grad_down[None]


def solution(mesh):
    rows = P("dp", None)
    weights = P("expert", "dp", None)
    return jax.shard_map(
        on_device,
        mesh=mesh,
        in_specs=(rows, rows, rows, rows, weights, weights, weights),
        out_specs=(rows, rows, rows, weights, weights, weights),
        check_vma=False,
    )
```

```python
import jax
import jax.numpy as jnp
from jax import lax
from jax.sharding import PartitionSpec as P

BF = jnp.bfloat16
F32 = jnp.float32
ZH, CORES, NX, NY, ZL = 4, 2, 4, 4, 2
BOTH = ("expert", "dp")
BASE, OVER = 16, 8
SLOTS = BASE + OVER
CELL, CUT = 2 * SLOTS, 2 * BASE


def linear(zh, core, x, y, zl):
    return (((zh * CORES + core) * NX + x) * NY + y) * ZL + zl


def moves(step):
    pairs = []
    for zh in range(ZH):
        for core in range(CORES):
            for x in range(NX):
                for y in range(NY):
                    for zl in range(ZL):
                        at = (zh, core, x, y, zl)
                        pairs.append((linear(*at), linear(*step(*at))))
    return pairs


def along(first, shift):
    def step(zh, core, x, y, zl):
        if (core == 0) == first:
            return (zh, core, (x + shift) % NX, y, zl)
        return (zh, core, x, (y + shift) % NY, zl)

    return moves(step)


def planes(shift):
    return moves(lambda zh, core, x, y, zl: ((zh + shift) % ZH, core, x, y, zl))


TWIN = moves(lambda zh, core, x, y, zl: (zh, core, x, y, 1 - zl))
CORE = moves(lambda zh, core, x, y, zl: (zh, 1 - core, x, y, zl))
FIRST_UP, FIRST_DOWN = along(True, 1), along(True, -1)
SECOND_UP, SECOND_DOWN = along(False, 1), along(False, -1)


def send(value, pairs, name):
    with jax.named_scope(name):
        return lax.ppermute(value, BOTH, pairs)


def dot_nt(a, b):
    return lax.dot_general(a, b, (((1,), (1,)), ((), ())), preferred_element_type=F32)


def dot_nn(a, b):
    return lax.dot_general(a, b, (((1,), (0,)), ((), ())), preferred_element_type=F32)


def dot_tn(a, b):
    return lax.dot_general(a, b, (((0,), (0,)), ((), ())), preferred_element_type=F32)


def exact(a, b):
    return jnp.dot(a, b, preferred_element_type=F32, precision=lax.Precision.HIGHEST)


def join(own, twin):
    return jnp.concatenate([own[:, :BASE], twin[:, :BASE], own[:, BASE:], twin[:, BASE:]], axis=1)


def split(cell):
    own = jnp.concatenate([cell[:, :BASE], cell[:, CUT : CUT + OVER]], axis=1)
    twin = jnp.concatenate([cell[:, BASE:CUT], cell[:, CUT + OVER :]], axis=1)
    return own, twin


def tie(value, *others):
    return lax.optimization_barrier((value, *others))[0]


def on_device(tokens, cotangent, expert_ids, gate_values, w_gate, w_up, w_down):
    w_gate, w_up, w_down = w_gate[0], w_up[0], w_down[0]
    count = tokens.shape[0]
    mine = lax.axis_index("expert")
    core, plane = mine % CORES, mine // CORES
    pair = jnp.stack([mine, mine + 1 - 2 * core])
    matches = expert_ids[:, None, :] == pair[None, :, None]
    routed = jnp.any(matches, axis=2)
    weight = jnp.sum(jnp.where(matches, gate_values[:, None, :], 0.0), axis=2)
    position = jnp.cumsum(routed.astype(jnp.int32), axis=0) - 1
    hot = (position[-1, 0] >= BASE).astype(F32)
    base_slots = jnp.arange(BASE, dtype=jnp.int32)
    over_slots = BASE + OVER * core + jnp.arange(OVER, dtype=jnp.int32)
    none = jnp.zeros((count, BASE), bool)
    placing = [
        jnp.concatenate(
            [
                (routed[:, j, None] & (position[:, j, None] == base_slots)) if j == 0 else none,
                routed[:, j, None] & (position[:, j, None] == over_slots),
            ],
            axis=1,
        )
        for j in range(2)
    ]
    placed = (placing[0] | placing[1]).astype(BF)
    slot_weight = sum(jnp.sum(jnp.where(placing[j], weight[:, j, None], 0.0), axis=0) for j in range(2))
    row_inputs = dot_tn(placed, tokens).astype(BF)
    row_grads = (slot_weight[:, None] * dot_tn(placed, cotangent)).astype(BF)

    w_both = jnp.concatenate([w_gate, w_up])
    own = jnp.stack([row_inputs, row_grads])
    own = join(own, send(own, TWIN, "twin"))
    left, right = send(own, FIRST_UP, "first_left"), send(own, FIRST_DOWN, "first_right")
    far_x, far_g = send(right[0], FIRST_DOWN, "first_far_inputs"), send(left[1], FIRST_UP, "first_far_grads")
    own_a = jnp.stack([jnp.stack([f, left[a]]) for a, f in enumerate((far_x, far_g))])
    own_b = jnp.stack([right, own], axis=1)
    left_b, right_a = send(own_b, SECOND_UP, "left_b"), send(own_a, SECOND_DOWN, "right_a")
    left_a, right_b = send(own_a, SECOND_UP, "left_a"), send(own_b, SECOND_DOWN, "right_b")
    far_a, far_b = send(right_a, SECOND_DOWN, "far_a"), send(left_b, SECOND_UP, "far_b")

    def rows_of(cells):
        return cells.reshape(-1, cells.shape[-1])

    def forward(rows, cells):
        live = hot
        if cells:
            live = jnp.where(jnp.arange(rows.shape[0])[:, None] % CELL < CUT, 1.0, hot)
        g, u = jnp.split(dot_nt(rows, w_both), 2, axis=1)
        s = jax.nn.sigmoid(g)
        return live, g, u, s, (live * (g * s * u)).astype(BF)

    def backward(rows, live, g, u, s, hidden):
        h = live * dot_nt(rows, w_down)
        return hidden, jnp.concatenate([h * u * s * (1.0 + g * (1.0 - s)), h * (g * s)], axis=1).astype(BF)

    def partial(result):
        hidden, pre = result
        return dot_nn(hidden, w_down), dot_nn(pre, w_both)

    def others_of(inputs, grads, name):
        mine = jnp.stack([rows_of(jnp.concatenate([c[:, CUT:] for c in v])) for v in (inputs, grads)])
        return send(mine, CORE, name + "_core")

    def swap(mine, name):
        return send(mine, CORE, name + "_core_back").reshape(2, -1, CELL - CUT, mine.shape[-1])

    def below(rows):
        return jnp.pad(rows.astype(F32), ((0, 0), (CUT, 0), (0, 0)))

    near_x, near_g = zip(own_a, own_b, left_a, left_b, right_b)
    near_f = [forward(rows_of(x), True) for x in near_x]
    over = others_of(near_x, near_g, "near")
    near_b = [backward(rows_of(g), *f) for g, f in zip(near_g, near_f)]
    over_b = backward(over[1], *forward(over[0], False))
    near_mine = jnp.stack([v.astype(BF) for v in partial(over_b)])
    near_s = swap(near_mine, "near")

    def piece(half):
        return [
            v.reshape(2, CELL, -1) + below(near_s[a, 2 * half : 2 * half + 2] if half < 5 else far_s[a, :2])
            for a, v in enumerate(partial(near_b[half]))
        ]

    right_b = jnp.stack(piece(4)).astype(BF)
    left_a = jnp.stack(piece(2)).astype(BF)
    from_left_b, from_right_a = send(right_b, SECOND_UP, "right_sums"), send(left_a, SECOND_DOWN, "left_sums")

    far_a, far_b = tie(far_a, near_s, right_b, left_a), tie(far_b, near_s, right_b, left_a)
    right_a = tie(right_a, far_a)
    near_x, near_g = (*near_x, right_a[0]), (*near_g, right_a[1])
    near_b.append(backward(rows_of(right_a[1]), *forward(rows_of(right_a[0]), True)))
    far_x, far_g = zip(far_a, far_b)
    far_over = others_of((near_x[5], *far_x), (near_g[5], *far_g), "far")
    far_over_b = backward(far_over[1], *forward(far_over[0], False))
    far_s = swap(jnp.stack([v.astype(BF) for v in partial(far_over_b)]), "far")
    far_blocks = [backward(rows_of(g), *forward(rows_of(x), True)) for x, g in zip(far_x, far_g)]
    everything = [*near_b, over_b, *far_blocks, far_over_b]
    to_right, to_left, from_left_a, from_right_b = [], [], [], []
    for a in range(2):
        sums = [
            (partial(far_blocks[h])[a].reshape(2, CELL, -1) + below(far_s[a, 2 * h + 2 : 2 * h + 4])).astype(BF)
            for h in range(2)
        ]
        sums = [tie(v, from_left_b, from_right_a) for v in sums]
        to_right.append(send(sums[0], SECOND_UP, "far_sums"))
        to_left.append(send(sums[1], SECOND_DOWN, "far_sums"))
    for a in range(2):
        right_a = (piece(5)[a] + to_right[a].astype(F32)).astype(BF)
        left_b = (piece(3)[a] + to_left[a].astype(F32)).astype(BF)
        from_left_a.append(send(right_a, SECOND_UP, "right_sums"))
        from_right_b.append(send(left_b, SECOND_DOWN, "left_sums"))

    hidden, pre = (tie(jnp.concatenate([r[a] for r in everything]), *to_right, *to_left) for a in range(2))
    all_inputs = jnp.concatenate([*map(rows_of, near_x), over[0], *map(rows_of, far_x), far_over[0]])
    all_grads = jnp.concatenate([*map(rows_of, near_g), over[1], *map(rows_of, far_g), far_over[1]])
    grad_down = dot_tn(hidden, all_grads).astype(BF)
    grad_gate = dot_tn(pre[:, : w_gate.shape[0]], all_inputs).astype(BF)
    grad_up = dot_tn(pre[:, w_gate.shape[0] :], all_inputs).astype(BF)

    sum_a = [v + from_left_a[a].astype(F32) + from_right_a[a].astype(F32) for a, v in enumerate(piece(0))]
    sum_b = [v + from_left_b[a].astype(F32) + from_right_b[a].astype(F32) for a, v in enumerate(piece(1))]
    to_right = send(sum_a[0][0].astype(BF), FIRST_UP, "first_far_sums").astype(F32)
    to_left = send(sum_a[1][0].astype(BF), FIRST_DOWN, "first_far_sums").astype(F32)
    right = jnp.stack([sum_b[0][0] + to_right, sum_b[1][0]]).astype(BF)
    left = jnp.stack([sum_a[0][1], sum_a[1][1] + to_left]).astype(BF)
    from_left, from_right = send(right, FIRST_UP, "first_right_sums"), send(left, FIRST_DOWN, "first_left_sums")
    own_sum = jnp.stack([sum_b[0][1], sum_b[1][1]]) + from_left.astype(F32) + from_right.astype(F32)
    own_sum, twin_sum = split(own_sum)
    twin_sum = tie(twin_sum.astype(BF), grad_down, grad_gate, grad_up)
    out_rows, grad_rows = own_sum + send(twin_sum, TWIN, "twin_sums").astype(F32)

    part = count // (CORES * ZH)
    column = jnp.arange(count, dtype=jnp.int32)
    their_core = (core + column // (part * ZH)) % CORES
    their_plane = (plane + column // part) % ZH
    token = (their_core * ZH + their_plane) * part + column % part
    to_place = (jnp.arange(count, dtype=jnp.int32)[:, None] == token[None, :]).astype(BF)
    choose = dot_tn(to_place, placed)
    inner = exact(cotangent.astype(F32), out_rows.T)
    gate_grad = sum(
        jnp.where(matches[:, j, :], jnp.sum(jnp.where(placing[j], inner, 0.0), axis=1)[:, None], 0.0)
        for j in range(2)
    )
    high = lax.reduce_precision(gate_grad, 8, 7)
    parts = jnp.concatenate([high, gate_grad - high], axis=1).astype(BF)
    parts = jnp.pad(dot_tn(to_place, parts), ((0, 0), (0, 128 - 4)))
    term = jnp.stack(
        [
            jnp.concatenate([exact(choose * slot_weight, out_rows), parts], axis=1),
            jnp.concatenate([exact(choose, grad_rows), jnp.zeros_like(parts)], axis=1),
        ]
    )
    half = count // CORES
    term = term[:, :half] + send(term[:, half:].astype(BF), CORE, "core_sum").astype(F32)
    low, total = term.astype(BF), term[:, :part]
    for s in range(1, ZH):
        total = total + send(low[:, s * part : (s + 1) * part], planes(s), "planes_sum").astype(F32)
    total = total.astype(BF)
    term = jnp.concatenate([total] + [send(total, planes(-s), "planes") for s in range(1, ZH)], axis=1)
    term = jnp.concatenate([term, send(term, CORE, "core")], axis=1)
    width = tokens.shape[1]
    layer_out, input_grad = (dot_nn(to_place, term[a, :, :width]).astype(BF) for a in range(2))
    parts = dot_nn(to_place, term[0, :, width:])
    gate_grad = parts[:, :2] + parts[:, 2:4]
    return layer_out, input_grad, gate_grad, grad_gate[None], grad_up[None], grad_down[None]


def solution(mesh):
    rows = P("dp", None)
    weights = P("expert", "dp", None)
    return jax.shard_map(
        on_device,
        mesh=mesh,
        in_specs=(rows, rows, rows, rows, weights, weights, weights),
        out_specs=(rows, rows, rows, weights, weights, weights),
        check_vma=False,
    )
```
